32 devices in a mesh: section: 4 (over y, core), seq: 2 (over x), batch: 4 (over z).
Axes of the slice: x: 2, y: 2, z: 4, core: 2. Of those that a mesh axis runs over, the one named last changes fastest.
Arguments:
- latent: bfloat16 [4, 256, 3072], P('batch', 'seq'), may hold values from -6 to 6
- carried: bfloat16 [4, 256, 3072], P('batch', 'seq'), may hold values from -6 to 6
- samples: bfloat16 [4, 256, 3072], P('batch', 'seq'), may hold values from -6 to 6
- noise: bfloat16 [4, 256, 3072], P('batch', 'seq'), may hold values from -6 to 6
- gen_level: int32 [4], P('batch'), may hold values from 0 to 63
- score_level: int32 [4], P('batch'), may hold values from 0 to 63
- mod_table: float32 [4, 64, 3, 3072], P('section'), may hold values from -3 to 3
- qkv_weight: bfloat16 [4, 3072, 9216], P('section', ('seq', 'batch')), may hold values from -0.109375 to 0.109375
- out_weight: bfloat16 [4, 3072, 3072], P('section', None, ('seq', 'batch')), may hold values from -0.109375 to 0.109375
- query_gain: float32 [4, 128], P('section'), may hold values from 0.5 to 6
- key_gain: float32 [4, 128], P('section'), may hold values from 0.5 to 6
Outputs:
- block_out: bfloat16 [4, 4, 256, 3072], P('section', 'batch', 'seq')
- gen_grad: bfloat16 [4, 256, 3072], P('batch', 'seq', 'section')
The draws below stay inside these ranges and needn't reach their ends.
All inputs are finite; a program needn't handle non-finite values. Where the reference program divides by a largest or mean magnitude, that divisor is 1e-20 or more.
Results may differ from the reference program's by a relative error of at most 0.023.
The reference program's roundings to bfloat16 on the way (of `noised`, `modulated`, `weight` and `attended`) count: a program that leaves them out, or rounds other values in their place, can miss the bound.
Values may be sent and summed in bfloat16 or wider, within the bound.
A program may use at most 128 MiB of HBM per device.

```python
import math
import jax
import jax.numpy as jnp
from jax import lax

D = 3072
HEADS = 24
HD = 128
LEVELS = 64
LENGTH = 256
SAMPLES = 4
SECTIONS = 4


def draw_query_gain(key, part):
    key = jax.random.fold_in(key, 11)
    return jax.random.uniform(key, (SECTIONS, HD), jnp.float32, 0.5, 1.5)


def draw_key_gain(key, part):
    key = jax.random.fold_in(key, 23)
    return jax.random.uniform(key, (SECTIONS, HD), jnp.float32, 0.5, 1.5)


def with_ends(result, own_key, least, top_value):
    dims = result.shape
    index_at = [jax.random.randint(jax.random.fold_in(own_key, axis), (), 0, dims[axis]) for axis in range(len(dims))]
    result = result.at[tuple(index_at)].set(least)
    longest = dims.index(max(dims))
    index_at[longest] = (index_at[longest] + 1) % dims[longest]
    return result.at[tuple(index_at)].set(top_value)


def block_scale(rng, extent, split, smallest, largest):
    def one(axis_at, parts):
        steps = jax.random.uniform(jax.random.fold_in(jax.random.fold_in(rng, 6), axis_at), (parts,), jnp.float32, smallest / len(split), largest / len(split))
        return jnp.repeat(jnp.exp(steps), extent[axis_at] // parts).reshape((-1,) + (1,) * (len(extent) - axis_at - 1))

    level = one(*split[0])
    for cut in split[1:]:
        level = level * one(*cut)
    return level


def gaussian(key, dims, deviation, reach, cuts=(), dtype=jnp.bfloat16):
    array = deviation * jax.random.normal(key, dims, jnp.float32)
    if cuts:
        array = array * block_scale(key, dims, cuts, -0.22, 0.18)
    return jnp.clip(array, -reach, reach).astype(dtype)


def setup_inputs(seed: int = 0) -> dict:
    seeds = jax.random.split(jax.random.key(seed), 12)
    latent = gaussian(seeds[0], (SAMPLES, LENGTH, D), 1.0, 6.0, ((0, 4), (1, 2)))
    carried = gaussian(seeds[1], (SAMPLES, LENGTH, D), 1.0, 6.0, ((0, 4), (1, 2)))
    samples = gaussian(seeds[2], (SAMPLES, LENGTH, D), 1.0, 6.0, ((0, 4), (1, 2)))
    noise = gaussian(seeds[3], (SAMPLES, LENGTH, D), 1.0, 6.0, ((0, 4), (1, 2)))
    gen_level = with_ends(jax.random.randint(seeds[4], (SAMPLES,), 0, LEVELS), jax.random.fold_in(seeds[4], 1), 0, LEVELS - 1).astype(jnp.int32)
    score_level = with_ends(jax.random.randint(seeds[5], (SAMPLES,), 0, LEVELS), jax.random.fold_in(seeds[5], 1), 0, LEVELS - 1).astype(jnp.int32)
    mod_table = gaussian(seeds[6], (SECTIONS, LEVELS, 3, D), 0.5, 3.0, ((0, 4),), jnp.float32)
    qkv_weight = gaussian(seeds[7], (SECTIONS, D, 3 * HEADS * HD), D ** -0.5, 0.109375, ((0, 4), (1, 8)))
    out_weight = gaussian(seeds[8], (SECTIONS, HEADS * HD, D), (HEADS * HD) ** -0.5, 0.109375, ((0, 4), (2, 8)))
    query_gain = draw_query_gain(jax.random.fold_in(seeds[11], 71), 0)
    key_gain = draw_key_gain(jax.random.fold_in(seeds[11], 71), 0)
    return {"latent": latent, "carried": carried, "samples": samples, "noise": noise, "gen_level": gen_level, "score_level": score_level, "mod_table": mod_table, "qkv_weight": qkv_weight, "out_weight": out_weight, "query_gain": query_gain, "key_gain": key_gain}


norm_eps = 1e-06
mean_eps = 1e-05

def head_norm(raw, gain):
    power = lax.optimization_barrier(jnp.mean(raw * raw, axis=-1, keepdims=True))
    return (raw * lax.rsqrt(power + norm_eps) * gain).astype(jnp.bfloat16)

def block(source, picked, qkv_w, out_w, q_gain, k_gain):
    length = source.shape[0]
    data = source.astype(jnp.float32)
    center = data - lax.optimization_barrier(jnp.mean(data, axis=-1, keepdims=True))
    spread = lax.optimization_barrier(jnp.mean(center * center, axis=-1, keepdims=True))
    normed = center * lax.rsqrt(spread + norm_eps)
    modulated = (normed * (1.0 + picked[1]) + picked[0]).astype(jnp.bfloat16)
    qkv = jnp.dot(modulated, qkv_w, preferred_element_type=jnp.float32).reshape(length, 3, HEADS, HD)
    query = head_norm(qkv[:, 0], q_gain)
    keys = head_norm(qkv[:, 1], k_gain)
    values = qkv[:, 2].astype(jnp.bfloat16)
    scale = 1.0 / math.sqrt(HD)

    def one_head(args):
        q_head, k_head, v_head = args
        score = jnp.dot(q_head, k_head.T, preferred_element_type=jnp.float32) * scale
        top = lax.optimization_barrier(jnp.max(score, axis=-1, keepdims=True))
        weight = jnp.exp(score - top)
        total = lax.optimization_barrier(jnp.sum(weight, axis=-1, keepdims=True))
        mixed = jnp.dot(weight.astype(jnp.bfloat16), v_head, preferred_element_type=jnp.float32)
        return (mixed / total).astype(jnp.bfloat16)
    attended = lax.map(one_head, (query.transpose(1, 0, 2), keys.transpose(1, 0, 2), values.transpose(1, 0, 2)))
    attended = attended.transpose(1, 0, 2).reshape(length, HEADS * HD)
    proj = jnp.dot(attended, out_w, preferred_element_type=jnp.float32)
    return (data + picked[2] * proj).astype(jnp.bfloat16)

def reference(latent, carried, samples, noise, gen_level, score_level, mod_table, qkv_weight, out_weight, query_gain, key_gain):
    sigma = ((score_level.astype(jnp.float32) + 1.0) / LEVELS)[:, None, None]
    noised = ((1.0 - sigma) * samples.astype(jnp.float32) + sigma * noise.astype(jnp.float32)).astype(jnp.bfloat16)
    sources = [latent, carried, noised, noised]
    levels = [gen_level, gen_level, score_level, score_level]
    results = []
    for section in range(4):
        table = mod_table[section]

        def one_sample(args, section=section, table=table):
            source, level = args
            picked = table[level]
            return block(source, picked, qkv_weight[section], out_weight[section], query_gain[section], key_gain[section])
        results.append(lax.map(one_sample, (sources[section], levels[section])))
    block_out = jnp.stack(results)
    real = results[2].astype(jnp.float32)
    fake = results[3].astype(jnp.float32)
    spread = lax.optimization_barrier(jnp.mean(jnp.abs(samples.astype(jnp.float32) - real), axis=(1, 2), keepdims=True)) + mean_eps
    gen_grad = ((fake - real) / spread).astype(jnp.bfloat16)
    return (block_out, gen_grad)
```

```python
import functools
import math

import jax
import jax.numpy as jnp
from jax import lax
from jax.experimental import pallas as pl
from jax.experimental.pallas import tpu as pltpu
from jax.sharding import PartitionSpec as P

HEADS = 24
HD = 128
LEVELS = 64


norm_eps = 1e-06
mean_eps = 1e-05


def from_root(value, axis, source):
    kept = jnp.where(lax.axis_index(axis) == source, value, 0).astype(value.dtype)
    return lax.psum(kept, axis)


def modulate(source, table, level):
    levels = table.shape[0]
    onehot = (jnp.arange(levels, dtype=jnp.int32) == level).astype(jnp.float32)
    picked = jnp.dot(onehot[None, :], table.reshape(levels, -1), precision=lax.Precision.HIGHEST)
    picked = picked.reshape(3, -1)
    data = source.astype(jnp.float32)
    center = data - jnp.mean(data, axis=-1, keepdims=True)
    spread = jnp.mean(center * center, axis=-1, keepdims=True)
    normed = center * lax.rsqrt(spread + norm_eps)
    return ((normed * (1.0 + picked[1]) + picked[0]).astype(jnp.bfloat16), picked[2])


def head_norm(raw, gain):
    power = jnp.mean(raw * raw, axis=-1, keepdims=True)
    return (raw * lax.rsqrt(power + norm_eps) * gain).astype(jnp.bfloat16)


def pair_attention(stacked):
    width = stacked.shape[-1]
    length = stacked.shape[2]
    scale = 1.0 / math.sqrt(width)
    step = 512 if length > 512 and length % 512 == 0 else length

    def one_pair(args):
        q_head, k_head, v_head = args
        query_blocks = q_head.reshape(length // step, step, width)

        def one_block(query_block):
            score = jnp.dot(query_block, k_head.T, preferred_element_type=jnp.float32) * scale
            top = jnp.max(score, axis=-1, keepdims=True)
            weight = jnp.exp(score - top)
            total = jnp.sum(weight, axis=-1, keepdims=True)
            mixed = jnp.dot(weight.astype(jnp.bfloat16), v_head, preferred_element_type=jnp.float32)
            return (mixed / total).astype(jnp.bfloat16)

        return lax.map(one_block, query_blocks).reshape(length, width)

    return lax.map(one_pair, (stacked[0], stacked[1], stacked[2]))


def head_attention(query, keys, values):
    count, rows, heads, width = query.shape
    stacked = jnp.stack([query, keys, values])
    stacked = jnp.transpose(stacked, (0, 1, 3, 2, 4)).reshape(3, count * heads, rows, width)
    regrouped = lax.all_to_all(stacked, "seq", split_axis=1, concat_axis=2, tiled=True)
    mixed = pair_attention(regrouped)
    back = lax.all_to_all(mixed, "seq", split_axis=1, concat_axis=0, tiled=True)
    back = back.reshape(count, heads, rows, width)
    return jnp.transpose(back, (0, 2, 1, 3))


def scaled_gap(samples, real, fake):
    gap = samples.astype(jnp.float32) - real.astype(jnp.float32)
    cells = lax.axis_size("seq") * gap.shape[0] * gap.shape[1]
    total = lax.psum(jnp.sum(jnp.abs(gap)), "seq")
    spread = total / cells + mean_eps
    return ((fake.astype(jnp.float32) - real.astype(jnp.float32)) / spread).astype(jnp.bfloat16)


def by_batch(
    latent,
    carried,
    samples,
    noise,
    gen_level,
    score_level,
    mod_table,
    qkv_weight,
    out_weight,
    query_gain,
    key_gain,
):
    section = lax.axis_index("section")
    sigma = (score_level[0].astype(jnp.float32) + 1.0) / LEVELS
    noised = (
        (1.0 - sigma) * samples[0].astype(jnp.float32) + sigma * noise[0].astype(jnp.float32)
    ).astype(jnp.bfloat16)
    source = jnp.where(section == 0, latent[0], jnp.where(section == 1, carried[0], noised))
    level = jnp.where(section >= 2, score_level[0], gen_level[0])
    modulated, gate = modulate(source, mod_table[0], level)
    tok_rows = source.shape[0]
    qkv_local = qkv_weight[0]
    out_local = out_weight[0]
    q_gain = query_gain[0]
    k_gain = key_gain[0]
    groups = lax.axis_size("batch")
    local_rows = qkv_local.shape[0]
    own_heads = HEADS // groups
    mine = lax.all_to_all(
        qkv_local.reshape(local_rows, 3, HEADS, HD),
        "batch",
        split_axis=2,
        concat_axis=0,
        tiled=True,
    )
    mine = mine.reshape(local_rows * groups, 3 * own_heads * HD)
    everyone = lax.all_gather(modulated, "batch", axis=0, tiled=True)
    qkv = jnp.dot(
        everyone,
        lax.all_gather(mine, "seq", axis=0, tiled=True),
        preferred_element_type=jnp.float32,
    )
    qkv = qkv.reshape(groups, tok_rows, 3, own_heads, HD)
    query = head_norm(qkv[:, :, 0], q_gain)
    keys = head_norm(qkv[:, :, 1], k_gain)
    values = qkv[:, :, 2].astype(jnp.bfloat16)
    attended = head_attention(query, keys, values)
    attended = attended.reshape(groups * tok_rows, own_heads * HD)
    out_rows = lax.all_to_all(out_local, "batch", split_axis=0, concat_axis=1, tiled=True)
    out_rows = lax.all_gather(out_rows, "seq", axis=1, tiled=True)
    proj = lax.psum_scatter(
        jnp.dot(attended, out_rows, preferred_element_type=jnp.float32),
        "batch",
        scatter_dimension=0,
        tiled=True,
    )
    result = (source.astype(jnp.float32) + gate * proj).astype(jnp.bfloat16)
    real = from_root(result, "section", 2)
    fake = from_root(result, "section", 3)
    gen_grad = scaled_gap(samples[0], real, fake)
    col_width = gen_grad.shape[1] // lax.axis_size("section")
    own_cols = lax.dynamic_slice_in_dim(gen_grad, section * col_width, col_width, 1)
    return (result[None, None], own_cols[None])


MESH = pl.DeviceIdType.MESH


def greet(peers):
    barrier = pltpu.get_barrier_semaphore()
    for peer in peers:
        pl.semaphore_signal(barrier, inc=1, device_id=peer, device_id_type=MESH)
    pl.semaphore_wait(barrier, len(peers))


def group_peers(seqs, batches):
    section, seq, batch = (lax.axis_index(name) for name in ("section", "seq", "batch"))
    found = []
    for near in range(batches):
        for side in range(seqs):
            to_seq = lax.rem(seq + side, seqs)
            to_batch = lax.rem(batch + near, batches)
            back_seq = lax.rem(seq - side + seqs, seqs)
            back_batch = lax.rem(batch - near + batches, batches)
            found.append(((section, to_seq, to_batch), (to_seq, to_batch), (back_seq, back_batch)))
    return found


def attend_kernel(
    seqs, batches, w_ref, mod_ref, qg_ref, kg_ref, out_ref, wbuf, mbuf, acc, own_sem, w_send, w_recv, m_send, m_recv
):
    seq, batch = lax.axis_index("seq"), lax.axis_index("batch")
    groups = seqs * batches
    me = seq * batches + batch
    depth = w_ref.shape[0]
    width = w_ref.shape[1] // 3
    share = width // groups
    rows = mod_ref.shape[0]
    length = rows * seqs
    peers = group_peers(seqs, batches)
    greet([coords for coords, _, _ in peers[1:]])

    def columns(rank, part):
        return pl.ds(pl.multiple_of(part * width + rank * share, 128), share)

    my_rows = pl.ds(pl.multiple_of((batch * seqs + seq) * rows, rows), rows)
    copies = []
    for at, (coords, _, _) in enumerate(peers):
        if at == 0:
            continue
        copy = pltpu.make_async_remote_copy(
            mod_ref, mbuf.at[my_rows, :], m_send.at[at], m_recv.at[at], device_id=coords, device_id_type=MESH
        )
        copy.start()
        copies.append(copy)
    weights = []
    for at, (coords, (to_seq, to_batch), _) in enumerate(peers):
        rank = to_seq * batches + to_batch
        for part in range(3):
            source = w_ref.at[:, columns(rank, part)]
            target = wbuf.at[me, :, pl.ds(part * share, share)]
            if at == 0:
                copy = pltpu.make_async_copy(source, target, own_sem.at[part])
            else:
                copy = pltpu.make_async_remote_copy(
                    source,
                    target,
                    w_send.at[at, part],
                    w_recv.at[at, part],
                    device_id=coords,
                    device_id_type=MESH,
                )
            copy.start()
            weights.append(copy)
    mbuf[my_rows, :] = mod_ref[...]
    for copy in copies:
        copy.wait()
    for at, (_, _, (from_seq, from_batch)) in enumerate(peers):
        for part in range(3):
            weights[3 * at + part].wait()
        rank = from_seq * batches + from_batch
        deep = pl.ds(pl.multiple_of(rank * depth, 128), depth)

        @pl.loop(0, batches)
        def _(sample):
            these = pl.ds(pl.multiple_of(sample * length, length), length)
            term = jnp.dot(mbuf[these, deep], wbuf[rank], preferred_element_type=jnp.float32)
            if at == 0:
                acc[these, :] = term
            else:
                acc[these, :] += term

    scale = 1.0 / math.sqrt(HD)

    @pl.loop(0, batches)
    def _(sample):
        these = pl.ds(pl.multiple_of(sample * length, length), length)
        for head in range(share // HD):
            at = head * HD
            query = head_norm(acc[these, at : at + HD], qg_ref[...])
            keys = head_norm(acc[these, share + at : share + at + HD], kg_ref[...])
            values = acc[these, 2 * share + at : 2 * share + at + HD].astype(jnp.bfloat16)
            score = (
                lax.dot_general(query, keys, (((1,), (1,)), ((), ())), preferred_element_type=jnp.float32) * scale
            )
            top = jnp.max(score, axis=-1, keepdims=True)
            weight = jnp.exp(score - top)
            total = jnp.sum(weight, axis=-1, keepdims=True)
            mixed = jnp.dot(weight.astype(jnp.bfloat16), values, preferred_element_type=jnp.float32)
            out_ref[these, at : at + HD] = (mixed / total).astype(jnp.bfloat16)


def attend(seqs, batches, qkv_local, modulated, q_gain, k_gain):
    groups = seqs * batches
    depth, width = qkv_local.shape[0], qkv_local.shape[1] // 3
    share = width // groups
    rows = modulated.shape[0] * groups
    return pl.pallas_call(
        functools.partial(attend_kernel, seqs, batches),
        out_shape=jax.ShapeDtypeStruct((rows, share), jnp.bfloat16),
        in_specs=[pl.BlockSpec(memory_space=pl.ANY)] + [pl.BlockSpec(memory_space=pltpu.VMEM)] * 3,
        out_specs=pl.BlockSpec(memory_space=pltpu.VMEM),
        scratch_shapes=[
            pltpu.VMEM((groups, depth, 3 * share), jnp.bfloat16),
            pltpu.VMEM((rows, width), jnp.bfloat16),
            pltpu.VMEM((rows, 3 * share), jnp.float32),
            pltpu.SemaphoreType.DMA((3,)),
            pltpu.SemaphoreType.DMA((groups, 3)),
            pltpu.SemaphoreType.DMA((groups, 3)),
            pltpu.SemaphoreType.DMA((groups,)),
            pltpu.SemaphoreType.DMA((groups,)),
        ],
        compiler_params=pltpu.CompilerParams(
            collective_id=0, has_side_effects=True, vmem_limit_bytes=44 * 1024 * 1024
        ),
        name="attend",
    )(qkv_local, modulated, q_gain, k_gain)


def project_kernel(
    sections,
    seqs,
    batches,
    att_ref,
    w_ref,
    source_ref,
    gate_ref,
    samples_ref,
    out_ref,
    grad_ref,
    abuf,
    acc,
    psend,
    precv,
    cols,
    gaps,
    a_send,
    a_recv,
    p_send,
    p_recv,
    c_send,
    c_recv,
    g_send,
    g_recv,
):
    section, seq, batch = (lax.axis_index(name) for name in ("section", "seq", "batch"))
    me = seq * batches + batch
    rows, width = source_ref.shape
    share = w_ref.shape[1]
    depth = att_ref.shape[1]
    length = rows * seqs
    part = width // sections
    peers = group_peers(seqs, batches)
    across = []
    for far in range(sections):
        for side in range(seqs):
            to = (lax.rem(section + far, sections), lax.rem(seq + side, seqs))
            back = (lax.rem(section - far + sections, sections), lax.rem(seq - side + seqs, seqs))
            across.append(((to[0], to[1], batch), to, back, far, side))
    greet([p[0] for p in peers[1:]] + [p[0] for p in across if p[3] > 0])

    copies = []
    for at, (coords, _, _) in enumerate(peers):
        if at > 0:
            copy = pltpu.make_async_remote_copy(
                att_ref, abuf.at[me], a_send.at[at], a_recv.at[at], device_id=coords, device_id_type=MESH
            )
            copy.start()
            copies.append(copy)
    for at, (_, _, (from_seq, from_batch)) in enumerate(peers):
        rank = from_seq * batches + from_batch
        deep = pl.ds(pl.multiple_of(rank * depth, 128), depth)
        if at > 0:
            copies[at - 1].wait()

        @pl.loop(0, batches)
        def _(sample):
            these = pl.ds(pl.multiple_of(sample * length, length), length)
            block = att_ref[these, :] if at == 0 else abuf[rank, these, :]
            term = jnp.dot(block, w_ref[deep, :], preferred_element_type=jnp.float32)
            if at == 0:
                acc[these, :] = term
            else:
                acc[these, :] += term

    psend[...] = acc[...].astype(jnp.bfloat16)
    copies = []
    for at, (coords, (to_seq, to_batch), _) in enumerate(peers):
        theirs = pl.ds(pl.multiple_of((to_batch * seqs + to_seq) * rows, rows), rows)
        if at > 0:
            copy = pltpu.make_async_remote_copy(
                psend.at[theirs, :], precv.at[me], p_send.at[at], p_recv.at[at], device_id=coords, device_id_type=MESH
            )
            copy.start()
            copies.append(copy)
    my_rows = pl.ds(pl.multiple_of((batch * seqs + seq) * rows, rows), rows)
    for at, (_, _, (from_seq, from_batch)) in enumerate(peers):
        rank = from_seq * batches + from_batch
        here = pl.ds(pl.multiple_of(rank * share, 128), share)
        if at > 0:
            copies[at - 1].wait()
            proj = precv[rank].astype(jnp.float32)
        else:
            proj = acc[my_rows, :]
        out_ref[:, here] = (source_ref[:, here].astype(jnp.float32) + gate_ref[:, here] * proj).astype(jnp.bfloat16)

    gap = jnp.abs(samples_ref[...].astype(jnp.float32) - out_ref[...].astype(jnp.float32))
    mine = jnp.sum(gap)
    gaps[section, seq] = jnp.full(gaps.shape[2:], mine, jnp.float32)
    copies = []
    for at, (coords, to, back, far, side) in enumerate(across):
        if far > 0 and side == 0:
            theirs = pl.ds(pl.multiple_of(to[0] * part, 128), part)
            copy = pltpu.make_async_remote_copy(
                out_ref.at[:, theirs],
                cols.at[section],
                c_send.at[far],
                c_recv.at[far],
                device_id=coords,
                device_id_type=MESH,
            )
            copy.start()
            copies.append(copy)
        if at > 0:
            copy = pltpu.make_async_remote_copy(
                gaps.at[section, seq],
                gaps.at[section, seq],
                g_send.at[at],
                g_recv.at[at],
                device_id=coords,
                device_id_type=MESH,
            )
            copy.start()
            copies.append(copy)
    cols[section] = out_ref[:, pl.ds(pl.multiple_of(section * part, 128), part)]
    for copy in copies:
        copy.wait()
    total = gaps[2, 0][:1, :1]
    for side in range(1, seqs):
        total = total + gaps[2, side][:1, :1]
    spread = total / (length * width) + mean_eps
    real = cols[2].astype(jnp.float32)
    fake = cols[3].astype(jnp.float32)
    grad_ref[...] = ((fake - real) / spread).astype(jnp.bfloat16)


def project(sections, seqs, batches, attended, out_local, source, gate, samples):
    groups = seqs * batches
    rows, width = source.shape
    share = out_local.shape[1]
    depth = attended.shape[1]
    part = width // sections
    return pl.pallas_call(
        functools.partial(project_kernel, sections, seqs, batches),
        out_shape=(
            jax.ShapeDtypeStruct((rows, width), jnp.bfloat16),
            jax.ShapeDtypeStruct((rows, part), jnp.bfloat16),
        ),
        in_specs=[pl.BlockSpec(memory_space=pltpu.VMEM)] * 5,
        out_specs=(pl.BlockSpec(memory_space=pltpu.VMEM),) * 2,
        scratch_shapes=[
            pltpu.VMEM((groups, rows * groups, depth), jnp.bfloat16),
            pltpu.VMEM((rows * groups, share), jnp.float32),
            pltpu.VMEM((rows * groups, share), jnp.bfloat16),
            pltpu.VMEM((groups, rows, share), jnp.bfloat16),
            pltpu.VMEM((sections, rows, part), jnp.bfloat16),
            pltpu.VMEM((sections, seqs, 8, 128), jnp.float32),
            pltpu.SemaphoreType.DMA((groups,)),
            pltpu.SemaphoreType.DMA((groups,)),
            pltpu.SemaphoreType.DMA((groups,)),
            pltpu.SemaphoreType.DMA((groups,)),
            pltpu.SemaphoreType.DMA((sections,)),
            pltpu.SemaphoreType.DMA((sections,)),
            pltpu.SemaphoreType.DMA((sections * seqs,)),
            pltpu.SemaphoreType.DMA((sections * seqs,)),
        ],
        compiler_params=pltpu.CompilerParams(
            collective_id=1, has_side_effects=True, vmem_limit_bytes=44 * 1024 * 1024
        ),
        name="project",
    )(attended, out_local, source, gate, samples)


def pick_modulate(source, table, level):
    picked = lax.dynamic_index_in_dim(table, level, 0, keepdims=False)
    data = source.astype(jnp.float32)
    center = data - jnp.mean(data, axis=-1, keepdims=True)
    spread = jnp.mean(center * center, axis=-1, keepdims=True)
    normed = center * lax.rsqrt(spread + norm_eps)
    return ((normed * (1.0 + picked[1]) + picked[0]).astype(jnp.bfloat16), picked[2])


def by_heads(
    latent,
    carried,
    samples,
    noise,
    gen_level,
    score_level,
    mod_table,
    qkv_weight,
    out_weight,
    query_gain,
    key_gain,
):
    section = lax.axis_index("section")
    sections, seqs, batches = (lax.axis_size(name) for name in ("section", "seq", "batch"))
    sigma = (score_level[0].astype(jnp.float32) + 1.0) / LEVELS
    noised = (
        (1.0 - sigma) * samples[0].astype(jnp.float32) + sigma * noise[0].astype(jnp.float32)
    ).astype(jnp.bfloat16)
    source = jnp.where(section == 0, latent[0], jnp.where(section == 1, carried[0], noised))
    level = jnp.where(section >= 2, score_level[0], gen_level[0])
    modulated, gate = pick_modulate(source, mod_table[0], level)
    attended = attend(seqs, batches, qkv_weight[0], modulated, query_gain, key_gain)
    result, own_cols = project(
        sections, seqs, batches, attended, out_weight[0], source, gate[None], samples[0]
    )
    return (result[None, None], own_cols[None])


def solution(mesh):
    groups = mesh.shape["seq"] * mesh.shape["batch"]
    on_device = by_heads if HEADS % groups == 0 else by_batch
    return jax.shard_map(
        on_device,
        mesh=mesh,
        in_specs=(
            P("batch", "seq", None),
            P("batch", "seq", None),
            P("batch", "seq", None),
            P("batch", "seq", None),
            P("batch"),
            P("batch"),
            P("section", None, None, None),
            P("section", ("seq", "batch"), None),
            P("section", None, ("seq", "batch")),
            P("section", None),
            P("section", None),
        ),
        out_specs=(P("section", "batch", "seq", None), P("batch", "seq", "section")),
        check_vma=False,
    )
```

```python
import functools
import math

import jax
import jax.numpy as jnp
from jax import lax
from jax.experimental import pallas as pl
from jax.experimental.pallas import tpu as pltpu
from jax.sharding import PartitionSpec as P

HEADS = 24
HD = 128
LEVELS = 64


norm_eps = 1e-06
mean_eps = 1e-05


def from_root(value, axis, source):
    kept = jnp.where(lax.axis_index(axis) == source, value, 0).astype(value.dtype)
    return lax.psum(kept, axis)


def modulate(source, table, level):
    levels = table.shape[0]
    onehot = (jnp.arange(levels, dtype=jnp.int32) == level).astype(jnp.float32)
    picked = jnp.dot(onehot[None, :], table.reshape(levels, -1), precision=lax.Precision.HIGHEST)
    picked = picked.reshape(3, -1)
    data = source.astype(jnp.float32)
    center = data - jnp.mean(data, axis=-1, keepdims=True)
    spread = jnp.mean(center * center, axis=-1, keepdims=True)
    normed = center * lax.rsqrt(spread + norm_eps)
    return ((normed * (1.0 + picked[1]) + picked[0]).astype(jnp.bfloat16), picked[2])


def head_norm(raw, gain):
    power = jnp.mean(raw * raw, axis=-1, keepdims=True)
    return (raw * lax.rsqrt(power + norm_eps) * gain).astype(jnp.bfloat16)


def pair_attention(stacked):
    width = stacked.shape[-1]
    length = stacked.shape[2]
    scale = 1.0 / math.sqrt(width)
    step = 512 if length > 512 and length % 512 == 0 else length

    def one_pair(args):
        q_head, k_head, v_head = args
        query_blocks = q_head.reshape(length // step, step, width)

        def one_block(query_block):
            score = jnp.dot(query_block, k_head.T, preferred_element_type=jnp.float32) * scale
            top = jnp.max(score, axis=-1, keepdims=True)
            weight = jnp.exp(score - top)
            total = jnp.sum(weight, axis=-1, keepdims=True)
            mixed = jnp.dot(weight.astype(jnp.bfloat16), v_head, preferred_element_type=jnp.float32)
            return (mixed / total).astype(jnp.bfloat16)

        return lax.map(one_block, query_blocks).reshape(length, width)

    return lax.map(one_pair, (stacked[0], stacked[1], stacked[2]))


def head_attention(query, keys, values):
    count, rows, heads, width = query.shape
    stacked = jnp.stack([query, keys, values])
    stacked = jnp.transpose(stacked, (0, 1, 3, 2, 4)).reshape(3, count * heads, rows, width)
    regrouped = lax.all_to_all(stacked, "seq", split_axis=1, concat_axis=2, tiled=True)
    mixed = pair_attention(regrouped)
    back = lax.all_to_all(mixed, "seq", split_axis=1, concat_axis=0, tiled=True)
    back = back.reshape(count, heads, rows, width)
    return jnp.transpose(back, (0, 2, 1, 3))


def scaled_gap(samples, real, fake):
    gap = samples.astype(jnp.float32) - real.astype(jnp.float32)
    cells = lax.axis_size("seq") * gap.shape[0] * gap.shape[1]
    total = lax.psum(jnp.sum(jnp.abs(gap)), "seq")
    spread = total / cells + mean_eps
    return ((fake.astype(jnp.float32) - real.astype(jnp.float32)) / spread).astype(jnp.bfloat16)


def by_batch(
    latent,
    carried,
    samples,
    noise,
    gen_level,
    score_level,
    mod_table,
    qkv_weight,
    out_weight,
    query_gain,
    key_gain,
):
    section = lax.axis_index("section")
    sigma = (score_level[0].astype(jnp.float32) + 1.0) / LEVELS
    noised = (
        (1.0 - sigma) * samples[0].astype(jnp.float32) + sigma * noise[0].astype(jnp.float32)
    ).astype(jnp.bfloat16)
    source = jnp.where(section == 0, latent[0], jnp.where(section == 1, carried[0], noised))
    level = jnp.where(section >= 2, score_level[0], gen_level[0])
    modulated, gate = modulate(source, mod_table[0], level)
    tok_rows = source.shape[0]
    qkv_local = qkv_weight[0]
    out_local = out_weight[0]
    q_gain = query_gain[0]
    k_gain = key_gain[0]
    groups = lax.axis_size("batch")
    local_rows = qkv_local.shape[0]
    own_heads = HEADS // groups
    mine = lax.all_to_all(
        qkv_local.reshape(local_rows, 3, HEADS, HD),
        "batch",
        split_axis=2,
        concat_axis=0,
        tiled=True,
    )
    mine = mine.reshape(local_rows * groups, 3 * own_heads * HD)
    everyone = lax.all_gather(modulated, "batch", axis=0, tiled=True)
    qkv = jnp.dot(
        everyone,
        lax.all_gather(mine, "seq", axis=0, tiled=True),
        preferred_element_type=jnp.float32,
    )
    qkv = qkv.reshape(groups, tok_rows, 3, own_heads, HD)
    query = head_norm(qkv[:, :, 0], q_gain)
    keys = head_norm(qkv[:, :, 1], k_gain)
    values = qkv[:, :, 2].astype(jnp.bfloat16)
    attended = head_attention(query, keys, values)
    attended = attended.reshape(groups * tok_rows, own_heads * HD)
    out_rows = lax.all_to_all(out_local, "batch", split_axis=0, concat_axis=1, tiled=True)
    out_rows = lax.all_gather(out_rows, "seq", axis=1, tiled=True)
    proj = lax.psum_scatter(
        jnp.dot(attended, out_rows, preferred_element_type=jnp.float32),
        "batch",
        scatter_dimension=0,
        tiled=True,
    )
    result = (source.astype(jnp.float32) + gate * proj).astype(jnp.bfloat16)
    real = from_root(result, "section", 2)
    fake = from_root(result, "section", 3)
    gen_grad = scaled_gap(samples[0], real, fake)
    col_width = gen_grad.shape[1] // lax.axis_size("section")
    own_cols = lax.dynamic_slice_in_dim(gen_grad, section * col_width, col_width, 1)
    return (result[None, None], own_cols[None])


MESH = pl.DeviceIdType.MESH


def greet(peers):
    barrier = pltpu.get_barrier_semaphore()
    for peer in peers:
        pl.semaphore_signal(barrier, inc=1, device_id=peer, device_id_type=MESH)
    pl.semaphore_wait(barrier, len(peers))


def group_peers(seqs, batches):
    section, seq, batch = (lax.axis_index(name) for name in ("section", "seq", "batch"))
    found = []
    for near in range(batches):
        for side in range(seqs):
            to_seq = lax.rem(seq + side, seqs)
            to_batch = lax.rem(batch + near, batches)
            back_seq = lax.rem(seq - side + seqs, seqs)
            back_batch = lax.rem(batch - near + batches, batches)
            found.append(((section, to_seq, to_batch), (to_seq, to_batch), (back_seq, back_batch)))
    return found


def gather_slots(seqs, batches):
    return 2 * batches * (1 + 2 * seqs) + 2 * seqs


def gather(seqs, batches, own, place, cut, send_sem, recv_sem, between=lambda step: None):
    section, seq, batch = (lax.axis_index(name) for name in ("section", "seq", "batch"))
    rows = own.shape[0]
    slots = {}
    sent = []

    def remote(source, target, key, to_seq, to_batch):
        slot = slots.setdefault(key, len(slots))
        return pltpu.make_async_remote_copy(
            source,
            target,
            send_sem.at[slot],
            recv_sem.at[slot],
            device_id=(section, to_seq, to_batch),
            device_id_type=MESH,
        )

    def send(ok, make):
        if ok is None:
            make().start()
        else:
            pl.when(ok)(lambda: make().start())
        sent.append((ok, make))

    def bounds(stream):
        return (0, cut) if stream == 0 else (cut, rows)

    def owner(stream):
        return seq if stream <= 1 else lax.rem(seq - (stream - 1) + seqs, seqs)

    def push(stream, right, step):
        if step >= batches:
            return
        index = batch - (step - 1) if right else batch + (step - 1)
        ok = (index >= 0) & (batch + 1 < batches) if right else (index < batches) & (batch >= 1)
        low, high = bounds(stream)

        def make():
            target = place(owner(stream), index, low, high)
            source = own.at[low:high] if step == 1 and stream <= 1 else target
            return remote(source, target, (stream, right, step), seq, batch + 1 if right else batch - 1)

        send(ok, make)

    def arrived(stream, right, step):
        index = batch - step if right else batch + step
        ok = index >= 0 if right else index < batches
        target = place(owner(stream), index, *bounds(stream))
        pl.when(ok)(lambda: remote(target, target, (stream, right, step), seq, batch).wait_recv())

    def over(right, step):
        index = batch - step if right else batch + step
        ok = None if step == 0 else (index >= 0 if right else index < batches)
        for side in range(1, seqs):

            def make(side=side):
                target = place(seq, index, 0, cut)
                source = own.at[0:cut] if step == 0 else target
                return remote(source, target, ("over", side, right, step), lax.rem(seq + side, seqs), batch)

            send(ok, make)

    def came_over(right, step):
        index = batch - step if right else batch + step
        for side in range(1, seqs):
            target = place(lax.rem(seq - side + seqs, seqs), index, 0, cut)
            copy = remote(target, target, ("over", side, right, step), seq, batch)
            if step == 0:
                copy.wait_recv()
            else:
                pl.when(index >= 0 if right else index < batches)(copy.wait_recv)

    late = list(range(1, seqs + 1)) if cut < rows else []
    if late:
        for side in range(1, seqs):

            def make(side=side):
                target = place(seq, batch, cut, rows)
                return remote(own.at[cut:rows], target, ("first", side), lax.rem(seq + side, seqs), batch)

            send(None, make)
    for stream in [0] + late[:1]:
        for right in (True, False):
            push(stream, right, 1)
    over(True, 0)
    for side in late[1:]:
        target = place(owner(side), batch, cut, rows)
        remote(target, target, ("first", side - 1), seq, batch).wait_recv()
        for right in (True, False):
            push(side, right, 1)
    for step in range(1, batches):
        between(step)
        for stream in [0] + late:
            for right in (True, False):
                arrived(stream, right, step)
                push(stream, right, step + 1)
                if stream == 0:
                    over(right, step)
    came_over(True, 0)
    for step in range(1, batches):
        for right in (True, False):
            came_over(right, step)
    for ok, make in sent:
        if ok is None:
            make().wait_send()
        else:
            pl.when(ok)(lambda make=make: make().wait_send())


def attend_kernel(
    seqs, batches, w_ref, mod_ref, qg_ref, kg_ref, out_ref, wbuf, mbuf, acc, own_sem, w_send, w_recv, m_send, m_recv
):
    seq, batch = lax.axis_index("seq"), lax.axis_index("batch")
    groups = seqs * batches
    me = seq * batches + batch
    depth = w_ref.shape[0]
    width = w_ref.shape[1] // 3
    share = width // groups
    rows = mod_ref.shape[0]
    length = rows * seqs
    peers = group_peers(seqs, batches)
    greet([coords for coords, _, _ in peers[1:]])

    def columns(rank, part):
        return pl.ds(pl.multiple_of(part * width + rank * share, 128), share)

    my_rows = pl.ds(pl.multiple_of((batch * seqs + seq) * rows, rows), rows)
    mbuf[my_rows, :] = mod_ref[...]
    weights = {}

    def launch(ats):
        for at in ats:
            coords, (to_seq, to_batch), _ = peers[at]
            rank = to_seq * batches + to_batch
            for part in range(3):
                source = w_ref.at[:, columns(rank, part)]
                target = wbuf.at[me, :, pl.ds(part * share, share)]
                if at == 0:
                    copy = pltpu.make_async_copy(source, target, own_sem.at[part])
                else:
                    copy = pltpu.make_async_remote_copy(
                        source,
                        target,
                        w_send.at[at, part],
                        w_recv.at[at, part],
                        device_id=coords,
                        device_id_type=MESH,
                    )
                copy.start()
                weights[at, part] = copy

    def place(from_seq, from_batch, low, high):
        first = pl.multiple_of((from_batch * seqs + from_seq) * rows + low, 16)
        return mbuf.at[pl.ds(first, high - low), :]

    def between(step):
        if step == 1:
            launch(list(range(len(peers)))[::-1])

    gather(seqs, batches, mod_ref, place, rows, m_send, m_recv, between)
    for at, (_, _, (from_seq, from_batch)) in enumerate(peers):
        for part in range(3):
            weights[at, part].wait()
        rank = from_seq * batches + from_batch
        deep = pl.ds(pl.multiple_of(rank * depth, 128), depth)

        @pl.loop(0, batches)
        def _(sample):
            these = pl.ds(pl.multiple_of(sample * length, length), length)
            term = jnp.dot(mbuf[these, deep], wbuf[rank], preferred_element_type=jnp.float32)
            if at == 0:
                acc[these, :] = term
            else:
                acc[these, :] += term

    scale = 1.0 / math.sqrt(HD)

    @pl.loop(0, batches)
    def _(sample):
        these = pl.ds(pl.multiple_of(sample * length, length), length)
        for head in range(share // HD):
            at = head * HD
            query = head_norm(acc[these, at : at + HD], qg_ref[...])
            keys = head_norm(acc[these, share + at : share + at + HD], kg_ref[...])
            values = acc[these, 2 * share + at : 2 * share + at + HD].astype(jnp.bfloat16)
            score = (
                lax.dot_general(query, keys, (((1,), (1,)), ((), ())), preferred_element_type=jnp.float32) * scale
            )
            top = jnp.max(score, axis=-1, keepdims=True)
            weight = jnp.exp(score - top)
            total = jnp.sum(weight, axis=-1, keepdims=True)
            mixed = jnp.dot(weight.astype(jnp.bfloat16), values, preferred_element_type=jnp.float32)
            out_ref[these, at : at + HD] = (mixed / total).astype(jnp.bfloat16)


def attend(seqs, batches, qkv_local, modulated, q_gain, k_gain):
    groups = seqs * batches
    depth, width = qkv_local.shape[0], qkv_local.shape[1] // 3
    share = width // groups
    rows = modulated.shape[0] * groups
    return pl.pallas_call(
        functools.partial(attend_kernel, seqs, batches),
        out_shape=jax.ShapeDtypeStruct((rows, share), jnp.bfloat16),
        in_specs=[pl.BlockSpec(memory_space=pl.ANY)] + [pl.BlockSpec(memory_space=pltpu.VMEM)] * 3,
        out_specs=pl.BlockSpec(memory_space=pltpu.VMEM),
        scratch_shapes=[
            pltpu.VMEM((groups, depth, 3 * share), jnp.bfloat16),
            pltpu.VMEM((rows, width), jnp.bfloat16),
            pltpu.VMEM((rows, 3 * share), jnp.float32),
            pltpu.SemaphoreType.DMA((3,)),
            pltpu.SemaphoreType.DMA((groups, 3)),
            pltpu.SemaphoreType.DMA((groups, 3)),
            pltpu.SemaphoreType.DMA((gather_slots(seqs, batches),)),
            pltpu.SemaphoreType.DMA((gather_slots(seqs, batches),)),
        ],
        compiler_params=pltpu.CompilerParams(
            collective_id=0, has_side_effects=True, vmem_limit_bytes=44 * 1024 * 1024
        ),
        name="attend",
    )(qkv_local, modulated, q_gain, k_gain)


def project_kernel(
    sections,
    seqs,
    batches,
    att_ref,
    w_ref,
    source_ref,
    gate_ref,
    samples_ref,
    out_ref,
    grad_ref,
    abuf,
    acc,
    psend,
    precv,
    cols,
    gaps,
    a_send,
    a_recv,
    p_send,
    p_recv,
    c_send,
    c_recv,
    g_send,
    g_recv,
):
    section, seq, batch = (lax.axis_index(name) for name in ("section", "seq", "batch"))
    me = seq * batches + batch
    rows, width = source_ref.shape
    share = w_ref.shape[1]
    depth = att_ref.shape[1]
    length = rows * seqs
    part = width // sections
    peers = group_peers(seqs, batches)
    across = []
    for far in range(sections):
        for side in range(seqs):
            to = (lax.rem(section + far, sections), lax.rem(seq + side, seqs))
            back = (lax.rem(section - far + sections, sections), lax.rem(seq - side + seqs, seqs))
            across.append(((to[0], to[1], batch), to, back, far, side))
    greet([p[0] for p in peers[1:]] + [p[0] for p in across if p[3] > 0])

    def place(from_seq, from_batch, low, high):
        return abuf.at[from_seq * batches + from_batch, low:high, :]

    gather(seqs, batches, att_ref, place, att_ref.shape[0] // 2, a_send, a_recv)
    for at, (_, _, (from_seq, from_batch)) in enumerate(peers):
        rank = from_seq * batches + from_batch
        deep = pl.ds(pl.multiple_of(rank * depth, 128), depth)

        @pl.loop(0, batches)
        def _(sample):
            these = pl.ds(pl.multiple_of(sample * length, length), length)
            block = att_ref[these, :] if at == 0 else abuf[rank, these, :]
            term = jnp.dot(block, w_ref[deep, :], preferred_element_type=jnp.float32)
            if at == 0:
                acc[these, :] = term
            else:
                acc[these, :] += term

    psend[...] = acc[...].astype(jnp.bfloat16)
    copies = []
    for at, (coords, (to_seq, to_batch), _) in enumerate(peers):
        theirs = pl.ds(pl.multiple_of((to_batch * seqs + to_seq) * rows, rows), rows)
        if at > 0:
            copy = pltpu.make_async_remote_copy(
                psend.at[theirs, :], precv.at[me], p_send.at[at], p_recv.at[at], device_id=coords, device_id_type=MESH
            )
            copy.start()
            copies.append(copy)
    my_rows = pl.ds(pl.multiple_of((batch * seqs + seq) * rows, rows), rows)
    for at, (_, _, (from_seq, from_batch)) in enumerate(peers):
        rank = from_seq * batches + from_batch
        here = pl.ds(pl.multiple_of(rank * share, 128), share)
        if at > 0:
            copies[at - 1].wait()
            proj = precv[rank].astype(jnp.float32)
        else:
            proj = acc[my_rows, :]
        out_ref[:, here] = (source_ref[:, here].astype(jnp.float32) + gate_ref[:, here] * proj).astype(jnp.bfloat16)

    gap = jnp.abs(samples_ref[...].astype(jnp.float32) - out_ref[...].astype(jnp.float32))
    mine = jnp.sum(gap)
    gaps[section, seq] = jnp.full(gaps.shape[2:], mine, jnp.float32)
    copies = []
    for at, (coords, to, back, far, side) in enumerate(across):
        if far > 0 and side == 0:
            theirs = pl.ds(pl.multiple_of(to[0] * part, 128), part)
            copy = pltpu.make_async_remote_copy(
                out_ref.at[:, theirs],
                cols.at[section],
                c_send.at[far],
                c_recv.at[far],
                device_id=coords,
                device_id_type=MESH,
            )
            copy.start()
            copies.append(copy)
        if at > 0:
            copy = pltpu.make_async_remote_copy(
                gaps.at[section, seq],
                gaps.at[section, seq],
                g_send.at[at],
                g_recv.at[at],
                device_id=coords,
                device_id_type=MESH,
            )
            copy.start()
            copies.append(copy)
    cols[section] = out_ref[:, pl.ds(pl.multiple_of(section * part, 128), part)]
    for copy in copies:
        copy.wait()
    total = gaps[2, 0][:1, :1]
    for side in range(1, seqs):
        total = total + gaps[2, side][:1, :1]
    spread = total / (length * width) + mean_eps
    real = cols[2].astype(jnp.float32)
    fake = cols[3].astype(jnp.float32)
    grad_ref[...] = ((fake - real) / spread).astype(jnp.bfloat16)


def project(sections, seqs, batches, attended, out_local, source, gate, samples):
    groups = seqs * batches
    rows, width = source.shape
    share = out_local.shape[1]
    depth = attended.shape[1]
    part = width // sections
    return pl.pallas_call(
        functools.partial(project_kernel, sections, seqs, batches),
        out_shape=(
            jax.ShapeDtypeStruct((rows, width), jnp.bfloat16),
            jax.ShapeDtypeStruct((rows, part), jnp.bfloat16),
        ),
        in_specs=[pl.BlockSpec(memory_space=pltpu.VMEM)] * 5,
        out_specs=(pl.BlockSpec(memory_space=pltpu.VMEM),) * 2,
        scratch_shapes=[
            pltpu.VMEM((groups, rows * groups, depth), jnp.bfloat16),
            pltpu.VMEM((rows * groups, share), jnp.float32),
            pltpu.VMEM((rows * groups, share), jnp.bfloat16),
            pltpu.VMEM((groups, rows, share), jnp.bfloat16),
            pltpu.VMEM((sections, rows, part), jnp.bfloat16),
            pltpu.VMEM((sections, seqs, 8, 128), jnp.float32),
            pltpu.SemaphoreType.DMA((gather_slots(seqs, batches),)),
            pltpu.SemaphoreType.DMA((gather_slots(seqs, batches),)),
            pltpu.SemaphoreType.DMA((groups,)),
            pltpu.SemaphoreType.DMA((groups,)),
            pltpu.SemaphoreType.DMA((sections,)),
            pltpu.SemaphoreType.DMA((sections,)),
            pltpu.SemaphoreType.DMA((sections * seqs,)),
            pltpu.SemaphoreType.DMA((sections * seqs,)),
        ],
        compiler_params=pltpu.CompilerParams(
            collective_id=1, has_side_effects=True, vmem_limit_bytes=44 * 1024 * 1024
        ),
        name="project",
    )(attended, out_local, source, gate, samples)


def pick_modulate(source, table, level):
    picked = lax.dynamic_index_in_dim(table, level, 0, keepdims=False)
    data = source.astype(jnp.float32)
    center = data - jnp.mean(data, axis=-1, keepdims=True)
    spread = jnp.mean(center * center, axis=-1, keepdims=True)
    normed = center * lax.rsqrt(spread + norm_eps)
    return ((normed * (1.0 + picked[1]) + picked[0]).astype(jnp.bfloat16), picked[2])


def by_heads(
    latent,
    carried,
    samples,
    noise,
    gen_level,
    score_level,
    mod_table,
    qkv_weight,
    out_weight,
    query_gain,
    key_gain,
):
    section = lax.axis_index("section")
    sections, seqs, batches = (lax.axis_size(name) for name in ("section", "seq", "batch"))
    sigma = (score_level[0].astype(jnp.float32) + 1.0) / LEVELS
    noised = (
        (1.0 - sigma) * samples[0].astype(jnp.float32) + sigma * noise[0].astype(jnp.float32)
    ).astype(jnp.bfloat16)
    source = jnp.where(section == 0, latent[0], jnp.where(section == 1, carried[0], noised))
    level = jnp.where(section >= 2, score_level[0], gen_level[0])
    modulated, gate = pick_modulate(source, mod_table[0], level)
    attended = attend(seqs, batches, qkv_weight[0], modulated, query_gain, key_gain)
    result, own_cols = project(
        sections, seqs, batches, attended, out_weight[0], source, gate[None], samples[0]
    )
    return (result[None, None], own_cols[None])


def solution(mesh):
    groups = mesh.shape["seq"] * mesh.shape["batch"]
    on_device = by_heads if HEADS % groups == 0 else by_batch
    return jax.shard_map(
        on_device,
        mesh=mesh,
        in_specs=(
            P("batch", "seq", None),
            P("batch", "seq", None),
            P("batch", "seq", None),
            P("batch", "seq", None),
            P("batch"),
            P("batch"),
            P("section", None, None, None),
            P("section", ("seq", "batch"), None),
            P("section", None, ("seq", "batch")),
            P("section", None),
            P("section", None),
        ),
        out_specs=(P("section", "batch", "seq", None), P("batch", "seq", "section")),
        check_vma=False,
    )
```

```python
import functools
import math

import jax
import jax.numpy as jnp
from jax import lax
from jax.experimental import pallas as pl
from jax.experimental.pallas import tpu as pltpu
from jax.sharding import PartitionSpec as P

HEADS = 24
HD = 128
LEVELS = 64


norm_eps = 1e-06
mean_eps = 1e-05


def from_root(value, axis, source):
    kept = jnp.where(lax.axis_index(axis) == source, value, 0).astype(value.dtype)
    return lax.psum(kept, axis)


def modulate(source, table, level):
    levels = table.shape[0]
    onehot = (jnp.arange(levels, dtype=jnp.int32) == level).astype(jnp.float32)
    picked = jnp.dot(onehot[None, :], table.reshape(levels, -1), precision=lax.Precision.HIGHEST)
    picked = picked.reshape(3, -1)
    data = source.astype(jnp.float32)
    center = data - jnp.mean(data, axis=-1, keepdims=True)
    spread = jnp.mean(center * center, axis=-1, keepdims=True)
    normed = center * lax.rsqrt(spread + norm_eps)
    return ((normed * (1.0 + picked[1]) + picked[0]).astype(jnp.bfloat16), picked[2])


def head_norm(raw, gain):
    power = jnp.mean(raw * raw, axis=-1, keepdims=True)
    return (raw * lax.rsqrt(power + norm_eps) * gain).astype(jnp.bfloat16)


def pair_attention(stacked):
    width = stacked.shape[-1]
    length = stacked.shape[2]
    scale = 1.0 / math.sqrt(width)
    step = 512 if length > 512 and length % 512 == 0 else length

    def one_pair(args):
        q_head, k_head, v_head = args
        query_blocks = q_head.reshape(length // step, step, width)

        def one_block(query_block):
            score = jnp.dot(query_block, k_head.T, preferred_element_type=jnp.float32) * scale
            top = jnp.max(score, axis=-1, keepdims=True)
            weight = jnp.exp(score - top)
            total = jnp.sum(weight, axis=-1, keepdims=True)
            mixed = jnp.dot(weight.astype(jnp.bfloat16), v_head, preferred_element_type=jnp.float32)
            return (mixed / total).astype(jnp.bfloat16)

        return lax.map(one_block, query_blocks).reshape(length, width)

    return lax.map(one_pair, (stacked[0], stacked[1], stacked[2]))


def head_attention(query, keys, values):
    count, rows, heads, width = query.shape
    stacked = jnp.stack([query, keys, values])
    stacked = jnp.transpose(stacked, (0, 1, 3, 2, 4)).reshape(3, count * heads, rows, width)
    regrouped = lax.all_to_all(stacked, "seq", split_axis=1, concat_axis=2, tiled=True)
    mixed = pair_attention(regrouped)
    back = lax.all_to_all(mixed, "seq", split_axis=1, concat_axis=0, tiled=True)
    back = back.reshape(count, heads, rows, width)
    return jnp.transpose(back, (0, 2, 1, 3))


def scaled_gap(samples, real, fake):
    gap = samples.astype(jnp.float32) - real.astype(jnp.float32)
    cells = lax.axis_size("seq") * gap.shape[0] * gap.shape[1]
    total = lax.psum(jnp.sum(jnp.abs(gap)), "seq")
    spread = total / cells + mean_eps
    return ((fake.astype(jnp.float32) - real.astype(jnp.float32)) / spread).astype(jnp.bfloat16)


def by_batch(
    latent,
    carried,
    samples,
    noise,
    gen_level,
    score_level,
    mod_table,
    qkv_weight,
    out_weight,
    query_gain,
    key_gain,
):
    section = lax.axis_index("section")
    sigma = (score_level[0].astype(jnp.float32) + 1.0) / LEVELS
    noised = (
        (1.0 - sigma) * samples[0].astype(jnp.float32) + sigma * noise[0].astype(jnp.float32)
    ).astype(jnp.bfloat16)
    source = jnp.where(section == 0, latent[0], jnp.where(section == 1, carried[0], noised))
    level = jnp.where(section >= 2, score_level[0], gen_level[0])
    modulated, gate = modulate(source, mod_table[0], level)
    tok_rows = source.shape[0]
    qkv_local = qkv_weight[0]
    out_local = out_weight[0]
    q_gain = query_gain[0]
    k_gain = key_gain[0]
    groups = lax.axis_size("batch")
    local_rows = qkv_local.shape[0]
    own_heads = HEADS // groups
    mine = lax.all_to_all(
        qkv_local.reshape(local_rows, 3, HEADS, HD),
        "batch",
        split_axis=2,
        concat_axis=0,
        tiled=True,
    )
    mine = mine.reshape(local_rows * groups, 3 * own_heads * HD)
    everyone = lax.all_gather(modulated, "batch", axis=0, tiled=True)
    qkv = jnp.dot(
        everyone,
        lax.all_gather(mine, "seq", axis=0, tiled=True),
        preferred_element_type=jnp.float32,
    )
    qkv = qkv.reshape(groups, tok_rows, 3, own_heads, HD)
    query = head_norm(qkv[:, :, 0], q_gain)
    keys = head_norm(qkv[:, :, 1], k_gain)
    values = qkv[:, :, 2].astype(jnp.bfloat16)
    attended = head_attention(query, keys, values)
    attended = attended.reshape(groups * tok_rows, own_heads * HD)
    out_rows = lax.all_to_all(out_local, "batch", split_axis=0, concat_axis=1, tiled=True)
    out_rows = lax.all_gather(out_rows, "seq", axis=1, tiled=True)
    proj = lax.psum_scatter(
        jnp.dot(attended, out_rows, preferred_element_type=jnp.float32),
        "batch",
        scatter_dimension=0,
        tiled=True,
    )
    result = (source.astype(jnp.float32) + gate * proj).astype(jnp.bfloat16)
    real = from_root(result, "section", 2)
    fake = from_root(result, "section", 3)
    gen_grad = scaled_gap(samples[0], real, fake)
    col_width = gen_grad.shape[1] // lax.axis_size("section")
    own_cols = lax.dynamic_slice_in_dim(gen_grad, section * col_width, col_width, 1)
    return (result[None, None], own_cols[None])


MESH = pl.DeviceIdType.MESH


def greet(peers):
    barrier = pltpu.get_barrier_semaphore()
    for peer in peers:
        pl.semaphore_signal(barrier, inc=1, device_id=peer, device_id_type=MESH)
    pl.semaphore_wait(barrier, len(peers))


def group_peers(seqs, batches):
    section, seq, batch = (lax.axis_index(name) for name in ("section", "seq", "batch"))
    found = []
    for near in range(batches):
        for side in range(seqs):
            to_seq = lax.rem(seq + side, seqs)
            to_batch = lax.rem(batch + near, batches)
            back_seq = lax.rem(seq - side + seqs, seqs)
            back_batch = lax.rem(batch - near + batches, batches)
            found.append(((section, to_seq, to_batch), (to_seq, to_batch), (back_seq, back_batch)))
    return found


def gather_slots(seqs, batches):
    return 2 * batches * (1 + 2 * seqs) + 2 * seqs


def gather(seqs, batches, own, place, cut, send_sem, recv_sem, between=lambda step: None):
    section, seq, batch = (lax.axis_index(name) for name in ("section", "seq", "batch"))
    rows = own.shape[0]
    slots = {}
    sent = []

    def remote(source, target, key, to_seq, to_batch):
        slot = slots.setdefault(key, len(slots))
        return pltpu.make_async_remote_copy(
            source,
            target,
            send_sem.at[slot],
            recv_sem.at[slot],
            device_id=(section, to_seq, to_batch),
            device_id_type=MESH,
        )

    def send(ok, make):
        if ok is None:
            make().start()
        else:
            pl.when(ok)(lambda: make().start())
        sent.append((ok, make))

    def bounds(stream):
        return (0, cut) if stream == 0 else (cut, rows)

    def owner(stream):
        return seq if stream <= 1 else lax.rem(seq - (stream - 1) + seqs, seqs)

    def push(stream, right, step):
        if step >= batches:
            return
        index = batch - (step - 1) if right else batch + (step - 1)
        ok = (index >= 0) & (batch + 1 < batches) if right else (index < batches) & (batch >= 1)
        low, high = bounds(stream)

        def make():
            target = place(owner(stream), index, low, high)
            source = own.at[low:high] if step == 1 and stream <= 1 else target
            return remote(source, target, (stream, right, step), seq, batch + 1 if right else batch - 1)

        send(ok, make)

    def arrived(stream, right, step):
        index = batch - step if right else batch + step
        ok = index >= 0 if right else index < batches
        target = place(owner(stream), index, *bounds(stream))
        pl.when(ok)(lambda: remote(target, target, (stream, right, step), seq, batch).wait_recv())

    def over(right, step):
        index = batch - step if right else batch + step
        ok = None if step == 0 else (index >= 0 if right else index < batches)
        for side in range(1, seqs):

            def make(side=side):
                target = place(seq, index, 0, cut)
                source = own.at[0:cut] if step == 0 else target
                return remote(source, target, ("over", side, right, step), lax.rem(seq + side, seqs), batch)

            send(ok, make)

    def came_over(right, step):
        index = batch - step if right else batch + step
        for side in range(1, seqs):
            target = place(lax.rem(seq - side + seqs, seqs), index, 0, cut)
            copy = remote(target, target, ("over", side, right, step), seq, batch)
            if step == 0:
                copy.wait_recv()
            else:
                pl.when(index >= 0 if right else index < batches)(copy.wait_recv)

    late = list(range(1, seqs + 1)) if cut < rows else []
    if late:
        for side in range(1, seqs):

            def make(side=side):
                target = place(seq, batch, cut, rows)
                return remote(own.at[cut:rows], target, ("first", side), lax.rem(seq + side, seqs), batch)

            send(None, make)
    for stream in [0] + late[:1]:
        for right in (True, False):
            push(stream, right, 1)
    over(True, 0)
    for side in late[1:]:
        target = place(owner(side), batch, cut, rows)
        remote(target, target, ("first", side - 1), seq, batch).wait_recv()
        for right in (True, False):
            push(side, right, 1)
    for step in range(1, batches):
        between(step)
        for stream in [0] + late:
            for right in (True, False):
                arrived(stream, right, step)
                push(stream, right, step + 1)
                if stream == 0:
                    over(right, step)
    came_over(True, 0)
    for step in range(1, batches):
        for right in (True, False):
            came_over(right, step)
    for ok, make in sent:
        if ok is None:
            make().wait_send()
        else:
            pl.when(ok)(lambda make=make: make().wait_send())


def attend_kernel(
    seqs, batches, w_ref, mod_ref, qg_ref, kg_ref, out_ref, wbuf, mbuf, own_sem, w_send, w_recv, m_send, m_recv
):
    seq, batch = lax.axis_index("seq"), lax.axis_index("batch")
    groups = seqs * batches
    me = seq * batches + batch
    depth = w_ref.shape[0]
    width = w_ref.shape[1] // 3
    share = width // groups
    rows = mod_ref.shape[0]
    length = rows * seqs
    peers = group_peers(seqs, batches)
    greet([coords for coords, _, _ in peers[1:]])

    heads = share // HD

    def columns(rank, part, head):
        return pl.ds(pl.multiple_of(part * width + rank * share + head * HD, 128), HD)

    my_rows = pl.ds(pl.multiple_of((batch * seqs + seq) * rows, rows), rows)
    mbuf[my_rows, :] = mod_ref[...]
    weights = {}

    def launch(head):
        for at in reversed(range(groups)):
            coords, (to_seq, to_batch), _ = peers[at]
            rank = to_seq * batches + to_batch
            for part in range(3):
                slot = 3 * head + part
                source = w_ref.at[:, columns(rank, part, head)]
                target = wbuf.at[pl.ds(pl.multiple_of(me * depth, 128), depth), pl.ds(slot * HD, HD)]
                if at == 0:
                    copy = pltpu.make_async_copy(source, target, own_sem.at[slot])
                else:
                    copy = pltpu.make_async_remote_copy(
                        source,
                        target,
                        w_send.at[at, slot],
                        w_recv.at[at, slot],
                        device_id=coords,
                        device_id_type=MESH,
                    )
                copy.start()
                weights[at, slot] = copy

    def place(from_seq, from_batch, low, high):
        first = pl.multiple_of((from_batch * seqs + from_seq) * rows + low, 16)
        return mbuf.at[pl.ds(first, high - low), :]

    def between(step):
        for head in range(heads * (step - 1) // (batches - 1), heads * step // (batches - 1)):
            launch(head)

    gather(seqs, batches, mod_ref, place, rows, m_send, m_recv, between)
    scale = 1.0 / math.sqrt(HD)
    for head in range(heads):
        for at in range(groups):
            for part in range(3):
                weights[at, 3 * head + part].wait()

        @pl.loop(0, batches)
        def _(sample):
            these = pl.ds(pl.multiple_of(sample * length, length), length)
            own = wbuf[:, 3 * head * HD : 3 * (head + 1) * HD]
            qkv = jnp.dot(mbuf[these, :], own, preferred_element_type=jnp.float32)
            query = head_norm(qkv[:, :HD], qg_ref[...])
            keys = head_norm(qkv[:, HD : 2 * HD], kg_ref[...])
            values = qkv[:, 2 * HD :].astype(jnp.bfloat16)
            score = (
                lax.dot_general(query, keys, (((1,), (1,)), ((), ())), preferred_element_type=jnp.float32) * scale
            )
            top = jnp.max(score, axis=-1, keepdims=True)
            weight = jnp.exp(score - top)
            total = jnp.sum(weight, axis=-1, keepdims=True)
            mixed = jnp.dot(weight.astype(jnp.bfloat16), values, preferred_element_type=jnp.float32)
            out_ref[these, head * HD : (head + 1) * HD] = (mixed / total).astype(jnp.bfloat16)


def attend(seqs, batches, qkv_local, modulated, q_gain, k_gain):
    groups = seqs * batches
    depth, width = qkv_local.shape[0], qkv_local.shape[1] // 3
    share = width // groups
    rows = modulated.shape[0] * groups
    return pl.pallas_call(
        functools.partial(attend_kernel, seqs, batches),
        out_shape=jax.ShapeDtypeStruct((rows, share), jnp.bfloat16),
        in_specs=[pl.BlockSpec(memory_space=pl.ANY)] + [pl.BlockSpec(memory_space=pltpu.VMEM)] * 3,
        out_specs=pl.BlockSpec(memory_space=pltpu.VMEM),
        scratch_shapes=[
            pltpu.VMEM((groups * depth, 3 * share), jnp.bfloat16),
            pltpu.VMEM((rows, width), jnp.bfloat16),
            pltpu.SemaphoreType.DMA((3 * share // HD,)),
            pltpu.SemaphoreType.DMA((groups, 3 * share // HD)),
            pltpu.SemaphoreType.DMA((groups, 3 * share // HD)),
            pltpu.SemaphoreType.DMA((gather_slots(seqs, batches),)),
            pltpu.SemaphoreType.DMA((gather_slots(seqs, batches),)),
        ],
        compiler_params=pltpu.CompilerParams(
            collective_id=0, has_side_effects=True, vmem_limit_bytes=44 * 1024 * 1024
        ),
        name="attend",
    )(qkv_local, modulated, q_gain, k_gain)


def project_kernel(
    sections,
    seqs,
    batches,
    att_ref,
    w_ref,
    source_ref,
    gate_ref,
    samples_ref,
    out_ref,
    grad_ref,
    abuf,
    psend,
    precv,
    cols,
    gaps,
    a_send,
    a_recv,
    p_send,
    p_recv,
    c_send,
    c_recv,
    g_send,
    g_recv,
):
    section, seq, batch = (lax.axis_index(name) for name in ("section", "seq", "batch"))
    me = seq * batches + batch
    rows, width = source_ref.shape
    share = w_ref.shape[1]
    depth = att_ref.shape[1]
    length = rows * seqs
    part = width // sections
    peers = group_peers(seqs, batches)
    across = []
    for far in range(sections):
        for side in range(seqs):
            to = (lax.rem(section + far, sections), lax.rem(seq + side, seqs))
            back = (lax.rem(section - far + sections, sections), lax.rem(seq - side + seqs, seqs))
            across.append(((to[0], to[1], batch), to, back, far, side))
    greet([p[0] for p in peers[1:]] + [p[0] for p in across if p[3] > 0])

    def place(from_seq, from_batch, low, high):
        first = pl.multiple_of((from_seq * batches + from_batch) * depth, 128)
        return abuf.at[low:high, pl.ds(first, depth)]

    abuf[:, pl.ds(pl.multiple_of(me * depth, 128), depth)] = att_ref[...]
    gather(seqs, batches, att_ref, place, att_ref.shape[0] // 2, a_send, a_recv)
    copies = {}
    for near in reversed(range(batches)):
        sample = lax.rem(batch + near, batches)
        these = pl.ds(pl.multiple_of(sample * length, length), length)
        psend[these, :] = jnp.dot(abuf[these, :], w_ref[...], preferred_element_type=jnp.float32).astype(jnp.bfloat16)
        for at in range(near * seqs, (near + 1) * seqs):
            coords, (to_seq, to_batch), _ = peers[at]
            theirs = pl.ds(pl.multiple_of((to_batch * seqs + to_seq) * rows, rows), rows)
            if at > 0:
                copies[at] = pltpu.make_async_remote_copy(
                    psend.at[theirs, :],
                    precv.at[me],
                    p_send.at[at],
                    p_recv.at[at],
                    device_id=coords,
                    device_id_type=MESH,
                )
                copies[at].start()
    my_rows = pl.ds(pl.multiple_of((batch * seqs + seq) * rows, rows), rows)
    for at, (_, _, (from_seq, from_batch)) in enumerate(peers):
        rank = from_seq * batches + from_batch
        here = pl.ds(pl.multiple_of(rank * share, 128), share)
        if at > 0:
            copies[at].wait()
            proj = precv[rank].astype(jnp.float32)
        else:
            proj = psend[my_rows, :].astype(jnp.float32)
        out_ref[:, here] = (source_ref[:, here].astype(jnp.float32) + gate_ref[:, here] * proj).astype(jnp.bfloat16)

    gap = jnp.abs(samples_ref[...].astype(jnp.float32) - out_ref[...].astype(jnp.float32))
    mine = jnp.sum(gap)
    gaps[section, seq] = jnp.full(gaps.shape[2:], mine, jnp.float32)
    copies = []
    for at, (coords, to, back, far, side) in enumerate(across):
        if far > 0 and side == 0:
            theirs = pl.ds(pl.multiple_of(to[0] * part, 128), part)
            copy = pltpu.make_async_remote_copy(
                out_ref.at[:, theirs],
                cols.at[section],
                c_send.at[far],
                c_recv.at[far],
                device_id=coords,
                device_id_type=MESH,
            )
            copy.start()
            copies.append(copy)
        if at > 0:
            copy = pltpu.make_async_remote_copy(
                gaps.at[section, seq],
                gaps.at[section, seq],
                g_send.at[at],
                g_recv.at[at],
                device_id=coords,
                device_id_type=MESH,
            )
            copy.start()
            copies.append(copy)
    cols[section] = out_ref[:, pl.ds(pl.multiple_of(section * part, 128), part)]
    for copy in copies:
        copy.wait()
    total = gaps[2, 0][:1, :1]
    for side in range(1, seqs):
        total = total + gaps[2, side][:1, :1]
    spread = total / (length * width) + mean_eps
    real = cols[2].astype(jnp.float32)
    fake = cols[3].astype(jnp.float32)
    grad_ref[...] = ((fake - real) / spread).astype(jnp.bfloat16)


def project(sections, seqs, batches, attended, out_local, source, gate, samples):
    groups = seqs * batches
    rows, width = source.shape
    share = out_local.shape[1]
    depth = attended.shape[1]
    part = width // sections
    return pl.pallas_call(
        functools.partial(project_kernel, sections, seqs, batches),
        out_shape=(
            jax.ShapeDtypeStruct((rows, width), jnp.bfloat16),
            jax.ShapeDtypeStruct((rows, part), jnp.bfloat16),
        ),
        in_specs=[pl.BlockSpec(memory_space=pltpu.VMEM)] * 5,
        out_specs=(pl.BlockSpec(memory_space=pltpu.VMEM),) * 2,
        scratch_shapes=[
            pltpu.VMEM((rows * groups, width), jnp.bfloat16),
            pltpu.VMEM((rows * groups, share), jnp.bfloat16),
            pltpu.VMEM((groups, rows, share), jnp.bfloat16),
            pltpu.VMEM((sections, rows, part), jnp.bfloat16),
            pltpu.VMEM((sections, seqs, 8, 128), jnp.float32),
            pltpu.SemaphoreType.DMA((gather_slots(seqs, batches),)),
            pltpu.SemaphoreType.DMA((gather_slots(seqs, batches),)),
            pltpu.SemaphoreType.DMA((groups,)),
            pltpu.SemaphoreType.DMA((groups,)),
            pltpu.SemaphoreType.DMA((sections,)),
            pltpu.SemaphoreType.DMA((sections,)),
            pltpu.SemaphoreType.DMA((sections * seqs,)),
            pltpu.SemaphoreType.DMA((sections * seqs,)),
        ],
        compiler_params=pltpu.CompilerParams(
            collective_id=1, has_side_effects=True, vmem_limit_bytes=44 * 1024 * 1024
        ),
        name="project",
    )(attended, out_local, source, gate, samples)


def pick_modulate(source, table, level):
    picked = lax.dynamic_index_in_dim(table, level, 0, keepdims=False)
    data = source.astype(jnp.float32)
    center = data - jnp.mean(data, axis=-1, keepdims=True)
    spread = jnp.mean(center * center, axis=-1, keepdims=True)
    normed = center * lax.rsqrt(spread + norm_eps)
    return ((normed * (1.0 + picked[1]) + picked[0]).astype(jnp.bfloat16), picked[2])


def by_heads(
    latent,
    carried,
    samples,
    noise,
    gen_level,
    score_level,
    mod_table,
    qkv_weight,
    out_weight,
    query_gain,
    key_gain,
):
    section = lax.axis_index("section")
    sections, seqs, batches = (lax.axis_size(name) for name in ("section", "seq", "batch"))
    sigma = (score_level[0].astype(jnp.float32) + 1.0) / LEVELS
    noised = (
        (1.0 - sigma) * samples[0].astype(jnp.float32) + sigma * noise[0].astype(jnp.float32)
    ).astype(jnp.bfloat16)
    source = jnp.where(section == 0, latent[0], jnp.where(section == 1, carried[0], noised))
    level = jnp.where(section >= 2, score_level[0], gen_level[0])
    modulated, gate = pick_modulate(source, mod_table[0], level)
    attended = attend(seqs, batches, qkv_weight[0], modulated, query_gain, key_gain)
    result, own_cols = project(
        sections, seqs, batches, attended, out_weight[0], source, gate[None], samples[0]
    )
    return (result[None, None], own_cols[None])


def solution(mesh):
    groups = mesh.shape["seq"] * mesh.shape["batch"]
    on_device = by_heads if HEADS % groups == 0 else by_batch
    return jax.shard_map(
        on_device,
        mesh=mesh,
        in_specs=(
            P("batch", "seq", None),
            P("batch", "seq", None),
            P("batch", "seq", None),
            P("batch", "seq", None),
            P("batch"),
            P("batch"),
            P("section", None, None, None),
            P("section", ("seq", "batch"), None),
            P("section", None, ("seq", "batch")),
            P("section", None),
            P("section", None),
        ),
        out_specs=(P("section", "batch", "seq", None), P("batch", "seq", "section")),
        check_vma=False,
    )
```

```python
import functools
import math

import jax
import jax.numpy as jnp
from jax import lax
from jax.experimental import pallas as pl
from jax.experimental.pallas import tpu as pltpu
from jax.sharding import PartitionSpec as P

HEADS = 24
HD = 128
LEVELS = 64


norm_eps = 1e-06
mean_eps = 1e-05


def from_root(value, axis, source):
    kept = jnp.where(lax.axis_index(axis) == source, value, 0).astype(value.dtype)
    return lax.psum(kept, axis)


def modulate(source, table, level):
    levels = table.shape[0]
    onehot = (jnp.arange(levels, dtype=jnp.int32) == level).astype(jnp.float32)
    picked = jnp.dot(onehot[None, :], table.reshape(levels, -1), precision=lax.Precision.HIGHEST)
    picked = picked.reshape(3, -1)
    data = source.astype(jnp.float32)
    center = data - jnp.mean(data, axis=-1, keepdims=True)
    spread = jnp.mean(center * center, axis=-1, keepdims=True)
    normed = center * lax.rsqrt(spread + norm_eps)
    return ((normed * (1.0 + picked[1]) + picked[0]).astype(jnp.bfloat16), picked[2])


def head_norm(raw, gain):
    power = jnp.mean(raw * raw, axis=-1, keepdims=True)
    return (raw * lax.rsqrt(power + norm_eps) * gain).astype(jnp.bfloat16)


def pair_attention(stacked):
    width = stacked.shape[-1]
    length = stacked.shape[2]
    scale = 1.0 / math.sqrt(width)
    step = 512 if length > 512 and length % 512 == 0 else length

    def one_pair(args):
        q_head, k_head, v_head = args
        query_blocks = q_head.reshape(length // step, step, width)

        def one_block(query_block):
            score = jnp.dot(query_block, k_head.T, preferred_element_type=jnp.float32) * scale
            top = jnp.max(score, axis=-1, keepdims=True)
            weight = jnp.exp(score - top)
            total = jnp.sum(weight, axis=-1, keepdims=True)
            mixed = jnp.dot(weight.astype(jnp.bfloat16), v_head, preferred_element_type=jnp.float32)
            return (mixed / total).astype(jnp.bfloat16)

        return lax.map(one_block, query_blocks).reshape(length, width)

    return lax.map(one_pair, (stacked[0], stacked[1], stacked[2]))


def head_attention(query, keys, values):
    count, rows, heads, width = query.shape
    stacked = jnp.stack([query, keys, values])
    stacked = jnp.transpose(stacked, (0, 1, 3, 2, 4)).reshape(3, count * heads, rows, width)
    regrouped = lax.all_to_all(stacked, "seq", split_axis=1, concat_axis=2, tiled=True)
    mixed = pair_attention(regrouped)
    back = lax.all_to_all(mixed, "seq", split_axis=1, concat_axis=0, tiled=True)
    back = back.reshape(count, heads, rows, width)
    return jnp.transpose(back, (0, 2, 1, 3))


def scaled_gap(samples, real, fake):
    gap = samples.astype(jnp.float32) - real.astype(jnp.float32)
    cells = lax.axis_size("seq") * gap.shape[0] * gap.shape[1]
    total = lax.psum(jnp.sum(jnp.abs(gap)), "seq")
    spread = total / cells + mean_eps
    return ((fake.astype(jnp.float32) - real.astype(jnp.float32)) / spread).astype(jnp.bfloat16)


def by_batch(
    latent,
    carried,
    samples,
    noise,
    gen_level,
    score_level,
    mod_table,
    qkv_weight,
    out_weight,
    query_gain,
    key_gain,
):
    section = lax.axis_index("section")
    sigma = (score_level[0].astype(jnp.float32) + 1.0) / LEVELS
    noised = (
        (1.0 - sigma) * samples[0].astype(jnp.float32) + sigma * noise[0].astype(jnp.float32)
    ).astype(jnp.bfloat16)
    source = jnp.where(section == 0, latent[0], jnp.where(section == 1, carried[0], noised))
    level = jnp.where(section >= 2, score_level[0], gen_level[0])
    modulated, gate = modulate(source, mod_table[0], level)
    tok_rows = source.shape[0]
    qkv_local = qkv_weight[0]
    out_local = out_weight[0]
    q_gain = query_gain[0]
    k_gain = key_gain[0]
    groups = lax.axis_size("batch")
    local_rows = qkv_local.shape[0]
    own_heads = HEADS // groups
    mine = lax.all_to_all(
        qkv_local.reshape(local_rows, 3, HEADS, HD),
        "batch",
        split_axis=2,
        concat_axis=0,
        tiled=True,
    )
    mine = mine.reshape(local_rows * groups, 3 * own_heads * HD)
    everyone = lax.all_gather(modulated, "batch", axis=0, tiled=True)
    qkv = jnp.dot(
        everyone,
        lax.all_gather(mine, "seq", axis=0, tiled=True),
        preferred_element_type=jnp.float32,
    )
    qkv = qkv.reshape(groups, tok_rows, 3, own_heads, HD)
    query = head_norm(qkv[:, :, 0], q_gain)
    keys = head_norm(qkv[:, :, 1], k_gain)
    values = qkv[:, :, 2].astype(jnp.bfloat16)
    attended = head_attention(query, keys, values)
    attended = attended.reshape(groups * tok_rows, own_heads * HD)
    out_rows = lax.all_to_all(out_local, "batch", split_axis=0, concat_axis=1, tiled=True)
    out_rows = lax.all_gather(out_rows, "seq", axis=1, tiled=True)
    proj = lax.psum_scatter(
        jnp.dot(attended, out_rows, preferred_element_type=jnp.float32),
        "batch",
        scatter_dimension=0,
        tiled=True,
    )
    result = (source.astype(jnp.float32) + gate * proj).astype(jnp.bfloat16)
    real = from_root(result, "section", 2)
    fake = from_root(result, "section", 3)
    gen_grad = scaled_gap(samples[0], real, fake)
    col_width = gen_grad.shape[1] // lax.axis_size("section")
    own_cols = lax.dynamic_slice_in_dim(gen_grad, section * col_width, col_width, 1)
    return (result[None, None], own_cols[None])


MESH = pl.DeviceIdType.MESH


def greet(peers):
    barrier = pltpu.get_barrier_semaphore()
    for peer in peers:
        pl.semaphore_signal(barrier, inc=1, device_id=peer, device_id_type=MESH)
    pl.semaphore_wait(barrier, len(peers))


def group_peers(seqs, batches):
    section, seq, batch = (lax.axis_index(name) for name in ("section", "seq", "batch"))
    found = []
    for near in range(batches):
        for side in range(seqs):
            to_seq = lax.rem(seq + side, seqs)
            to_batch = lax.rem(batch + near, batches)
            back_seq = lax.rem(seq - side + seqs, seqs)
            back_batch = lax.rem(batch - near + batches, batches)
            found.append(((section, to_seq, to_batch), (to_seq, to_batch), (back_seq, back_batch)))
    return found


def gather_slots(seqs, batches):
    return 2 * batches * (1 + 2 * seqs) + 2 * seqs


def gather(seqs, batches, own, place, cut, send_sem, recv_sem, between=lambda step: None):
    section, seq, batch = (lax.axis_index(name) for name in ("section", "seq", "batch"))
    rows = own.shape[0]
    slots = {}
    sent = []

    def remote(source, target, key, to_seq, to_batch):
        slot = slots.setdefault(key, len(slots))
        return pltpu.make_async_remote_copy(
            source,
            target,
            send_sem.at[slot],
            recv_sem.at[slot],
            device_id=(section, to_seq, to_batch),
            device_id_type=MESH,
        )

    def send(ok, make):
        if ok is None:
            make().start()
        else:
            pl.when(ok)(lambda: make().start())
        sent.append((ok, make))

    def bounds(stream):
        return (0, cut) if stream == 0 else (cut, rows)

    def owner(stream):
        return seq if stream <= 1 else lax.rem(seq - (stream - 1) + seqs, seqs)

    def push(stream, right, step):
        if step >= batches:
            return
        index = batch - (step - 1) if right else batch + (step - 1)
        ok = (index >= 0) & (batch + 1 < batches) if right else (index < batches) & (batch >= 1)
        low, high = bounds(stream)

        def make():
            target = place(owner(stream), index, low, high)
            source = own.at[low:high] if step == 1 and stream <= 1 else target
            return remote(source, target, (stream, right, step), seq, batch + 1 if right else batch - 1)

        send(ok, make)

    def arrived(stream, right, step):
        index = batch - step if right else batch + step
        ok = index >= 0 if right else index < batches
        target = place(owner(stream), index, *bounds(stream))
        pl.when(ok)(lambda: remote(target, target, (stream, right, step), seq, batch).wait_recv())

    def over(right, step):
        index = batch - step if right else batch + step
        ok = None if step == 0 else (index >= 0 if right else index < batches)
        for side in range(1, seqs):

            def make(side=side):
                target = place(seq, index, 0, cut)
                source = own.at[0:cut] if step == 0 else target
                return remote(source, target, ("over", side, right, step), lax.rem(seq + side, seqs), batch)

            send(ok, make)

    def came_over(right, step):
        index = batch - step if right else batch + step
        for side in range(1, seqs):
            target = place(lax.rem(seq - side + seqs, seqs), index, 0, cut)
            copy = remote(target, target, ("over", side, right, step), seq, batch)
            if step == 0:
                copy.wait_recv()
            else:
                pl.when(index >= 0 if right else index < batches)(copy.wait_recv)

    late = list(range(1, seqs + 1)) if cut < rows else []
    if late:
        for side in range(1, seqs):

            def make(side=side):
                target = place(seq, batch, cut, rows)
                return remote(own.at[cut:rows], target, ("first", side), lax.rem(seq + side, seqs), batch)

            send(None, make)
    for stream in [0] + late[:1]:
        for right in (True, False):
            push(stream, right, 1)
    over(True, 0)
    for side in late[1:]:
        target = place(owner(side), batch, cut, rows)
        remote(target, target, ("first", side - 1), seq, batch).wait_recv()
        for right in (True, False):
            push(side, right, 1)
    for step in range(1, batches):
        between(step)
        for stream in [0] + late:
            for right in (True, False):
                arrived(stream, right, step)
                push(stream, right, step + 1)
                if stream == 0:
                    over(right, step)
    came_over(True, 0)
    for step in range(1, batches):
        for right in (True, False):
            came_over(right, step)
    for ok, make in sent:
        if ok is None:
            make().wait_send()
        else:
            pl.when(ok)(lambda make=make: make().wait_send())


def attend_kernel(
    seqs, batches, w_ref, mod_ref, qg_ref, kg_ref, out_ref, wbuf, mbuf, own_sem, w_send, w_recv, m_send, m_recv
):
    seq, batch = lax.axis_index("seq"), lax.axis_index("batch")
    groups = seqs * batches
    me = seq * batches + batch
    depth = w_ref.shape[0]
    width = w_ref.shape[1] // 3
    share = width // groups
    rows = mod_ref.shape[0]
    length = rows * seqs
    peers = group_peers(seqs, batches)
    greet([coords for coords, _, _ in peers[1:]])

    heads = share // HD

    def columns(rank, part, head):
        return pl.ds(pl.multiple_of(part * width + rank * share + head * HD, 128), HD)

    my_rows = pl.ds(pl.multiple_of((batch * seqs + seq) * rows, rows), rows)
    mbuf[my_rows, :] = mod_ref[...]
    weights = {}

    def launch(head):
        for at in reversed(range(groups)):
            coords, (to_seq, to_batch), _ = peers[at]
            rank = to_seq * batches + to_batch
            for part in range(3):
                slot = 3 * head + part
                source = w_ref.at[:, columns(rank, part, head)]
                target = wbuf.at[pl.ds(pl.multiple_of(me * depth, 128), depth), pl.ds(slot * HD, HD)]
                if at == 0:
                    copy = pltpu.make_async_copy(source, target, own_sem.at[slot])
                else:
                    copy = pltpu.make_async_remote_copy(
                        source,
                        target,
                        w_send.at[at, slot],
                        w_recv.at[at, slot],
                        device_id=coords,
                        device_id_type=MESH,
                    )
                copy.start()
                weights[at, slot] = copy

    def place(from_seq, from_batch, low, high):
        first = pl.multiple_of((from_batch * seqs + from_seq) * rows + low, 16)
        return mbuf.at[pl.ds(first, high - low), :]

    def between(step):
        for head in range(heads * (step - 1) // (batches - 1), heads * step // (batches - 1)):
            launch(head)

    gather(seqs, batches, mod_ref, place, rows // 2, m_send, m_recv, between)
    scale = 1.0 / math.sqrt(HD)
    for head in range(heads):
        for at in range(groups):
            for part in range(3):
                weights[at, 3 * head + part].wait()

        @pl.loop(0, batches)
        def _(sample):
            these = pl.ds(pl.multiple_of(sample * length, length), length)
            own = wbuf[:, 3 * head * HD : 3 * (head + 1) * HD]
            qkv = jnp.dot(mbuf[these, :], own, preferred_element_type=jnp.float32)
            query = head_norm(qkv[:, :HD], qg_ref[...])
            keys = head_norm(qkv[:, HD : 2 * HD], kg_ref[...])
            values = qkv[:, 2 * HD :].astype(jnp.bfloat16)
            score = (
                lax.dot_general(query, keys, (((1,), (1,)), ((), ())), preferred_element_type=jnp.float32) * scale
            )
            top = jnp.max(score, axis=-1, keepdims=True)
            weight = jnp.exp(score - top)
            total = jnp.sum(weight, axis=-1, keepdims=True)
            mixed = jnp.dot(weight.astype(jnp.bfloat16), values, preferred_element_type=jnp.float32)
            out_ref[these, head * HD : (head + 1) * HD] = (mixed / total).astype(jnp.bfloat16)


def attend(seqs, batches, qkv_local, modulated, q_gain, k_gain):
    groups = seqs * batches
    depth, width = qkv_local.shape[0], qkv_local.shape[1] // 3
    share = width // groups
    rows = modulated.shape[0] * groups
    return pl.pallas_call(
        functools.partial(attend_kernel, seqs, batches),
        out_shape=jax.ShapeDtypeStruct((rows, share), jnp.bfloat16),
        in_specs=[pl.BlockSpec(memory_space=pl.ANY)] + [pl.BlockSpec(memory_space=pltpu.VMEM)] * 3,
        out_specs=pl.BlockSpec(memory_space=pltpu.VMEM),
        scratch_shapes=[
            pltpu.VMEM((groups * depth, 3 * share), jnp.bfloat16),
            pltpu.VMEM((rows, width), jnp.bfloat16),
            pltpu.SemaphoreType.DMA((3 * share // HD,)),
            pltpu.SemaphoreType.DMA((groups, 3 * share // HD)),
            pltpu.SemaphoreType.DMA((groups, 3 * share // HD)),
            pltpu.SemaphoreType.DMA((gather_slots(seqs, batches),)),
            pltpu.SemaphoreType.DMA((gather_slots(seqs, batches),)),
        ],
        compiler_params=pltpu.CompilerParams(
            collective_id=0, has_side_effects=True, vmem_limit_bytes=44 * 1024 * 1024
        ),
        name="attend",
    )(qkv_local, modulated, q_gain, k_gain)


def project_kernel(
    sections,
    seqs,
    batches,
    att_ref,
    w_ref,
    source_ref,
    gate_ref,
    samples_ref,
    out_ref,
    grad_ref,
    abuf,
    psend,
    precv,
    cols,
    gaps,
    a_send,
    a_recv,
    p_send,
    p_recv,
    c_send,
    c_recv,
    g_send,
    g_recv,
):
    section, seq, batch = (lax.axis_index(name) for name in ("section", "seq", "batch"))
    me = seq * batches + batch
    rows, width = source_ref.shape
    share = w_ref.shape[1]
    depth = att_ref.shape[1]
    length = rows * seqs
    part = width // sections
    peers = group_peers(seqs, batches)
    across = []
    for far in range(sections):
        for side in range(seqs):
            to = (lax.rem(section + far, sections), lax.rem(seq + side, seqs))
            back = (lax.rem(section - far + sections, sections), lax.rem(seq - side + seqs, seqs))
            across.append(((to[0], to[1], batch), to, back, far, side))
    greet([p[0] for p in peers[1:]] + [p[0] for p in across if p[3] > 0])

    def place(from_seq, from_batch, low, high):
        first = pl.multiple_of((from_seq * batches + from_batch) * depth, 128)
        return abuf.at[low:high, pl.ds(first, depth)]

    abuf[:, pl.ds(pl.multiple_of(me * depth, 128), depth)] = att_ref[...]
    gather(seqs, batches, att_ref, place, att_ref.shape[0] // 2, a_send, a_recv)
    copies = {}
    for near in reversed(range(batches)):
        sample = lax.rem(batch + near, batches)
        these = pl.ds(pl.multiple_of(sample * length, length), length)
        psend[these, :] = jnp.dot(abuf[these, :], w_ref[...], preferred_element_type=jnp.float32).astype(jnp.bfloat16)
        for at in range(near * seqs, (near + 1) * seqs):
            coords, (to_seq, to_batch), _ = peers[at]
            theirs = pl.ds(pl.multiple_of((to_batch * seqs + to_seq) * rows, rows), rows)
            if at > 0:
                copies[at] = pltpu.make_async_remote_copy(
                    psend.at[theirs, :],
                    precv.at[me],
                    p_send.at[at],
                    p_recv.at[at],
                    device_id=coords,
                    device_id_type=MESH,
                )
                copies[at].start()
    my_rows = pl.ds(pl.multiple_of((batch * seqs + seq) * rows, rows), rows)
    for at, (_, _, (from_seq, from_batch)) in enumerate(peers):
        rank = from_seq * batches + from_batch
        here = pl.ds(pl.multiple_of(rank * share, 128), share)
        if at > 0:
            copies[at].wait()
            proj = precv[rank].astype(jnp.float32)
        else:
            proj = psend[my_rows, :].astype(jnp.float32)
        out_ref[:, here] = (source_ref[:, here].astype(jnp.float32) + gate_ref[:, here] * proj).astype(jnp.bfloat16)

    gap = jnp.abs(samples_ref[...].astype(jnp.float32) - out_ref[...].astype(jnp.float32))
    mine = jnp.sum(gap)
    gaps[section, seq] = jnp.full(gaps.shape[2:], mine, jnp.float32)
    copies = []
    for at, (coords, to, back, far, side) in enumerate(across):
        if far > 0 and side == 0:
            theirs = pl.ds(pl.multiple_of(to[0] * part, 128), part)
            copy = pltpu.make_async_remote_copy(
                out_ref.at[:, theirs],
                cols.at[section],
                c_send.at[far],
                c_recv.at[far],
                device_id=coords,
                device_id_type=MESH,
            )
            copy.start()
            copies.append(copy)
        if at > 0:
            copy = pltpu.make_async_remote_copy(
                gaps.at[section, seq],
                gaps.at[section, seq],
                g_send.at[at],
                g_recv.at[at],
                device_id=coords,
                device_id_type=MESH,
            )
            copy.start()
            copies.append(copy)
    cols[section] = out_ref[:, pl.ds(pl.multiple_of(section * part, 128), part)]
    for copy in copies:
        copy.wait()
    total = gaps[2, 0][:1, :1]
    for side in range(1, seqs):
        total = total + gaps[2, side][:1, :1]
    spread = total / (length * width) + mean_eps
    real = cols[2].astype(jnp.float32)
    fake = cols[3].astype(jnp.float32)
    grad_ref[...] = ((fake - real) / spread).astype(jnp.bfloat16)


def project(sections, seqs, batches, attended, out_local, source, gate, samples):
    groups = seqs * batches
    rows, width = source.shape
    share = out_local.shape[1]
    depth = attended.shape[1]
    part = width // sections
    return pl.pallas_call(
        functools.partial(project_kernel, sections, seqs, batches),
        out_shape=(
            jax.ShapeDtypeStruct((rows, width), jnp.bfloat16),
            jax.ShapeDtypeStruct((rows, part), jnp.bfloat16),
        ),
        in_specs=[pl.BlockSpec(memory_space=pltpu.VMEM)] * 5,
        out_specs=(pl.BlockSpec(memory_space=pltpu.VMEM),) * 2,
        scratch_shapes=[
            pltpu.VMEM((rows * groups, width), jnp.bfloat16),
            pltpu.VMEM((rows * groups, share), jnp.bfloat16),
            pltpu.VMEM((groups, rows, share), jnp.bfloat16),
            pltpu.VMEM((sections, rows, part), jnp.bfloat16),
            pltpu.VMEM((sections, seqs, 8, 128), jnp.float32),
            pltpu.SemaphoreType.DMA((gather_slots(seqs, batches),)),
            pltpu.SemaphoreType.DMA((gather_slots(seqs, batches),)),
            pltpu.SemaphoreType.DMA((groups,)),
            pltpu.SemaphoreType.DMA((groups,)),
            pltpu.SemaphoreType.DMA((sections,)),
            pltpu.SemaphoreType.DMA((sections,)),
            pltpu.SemaphoreType.DMA((sections * seqs,)),
            pltpu.SemaphoreType.DMA((sections * seqs,)),
        ],
        compiler_params=pltpu.CompilerParams(
            collective_id=1, has_side_effects=True, vmem_limit_bytes=44 * 1024 * 1024
        ),
        name="project",
    )(attended, out_local, source, gate, samples)


def pick_modulate(source, table, level):
    picked = lax.dynamic_index_in_dim(table, level, 0, keepdims=False)
    data = source.astype(jnp.float32)
    center = data - jnp.mean(data, axis=-1, keepdims=True)
    spread = jnp.mean(center * center, axis=-1, keepdims=True)
    normed = center * lax.rsqrt(spread + norm_eps)
    return ((normed * (1.0 + picked[1]) + picked[0]).astype(jnp.bfloat16), picked[2])


def by_heads(
    latent,
    carried,
    samples,
    noise,
    gen_level,
    score_level,
    mod_table,
    qkv_weight,
    out_weight,
    query_gain,
    key_gain,
):
    section = lax.axis_index("section")
    sections, seqs, batches = (lax.axis_size(name) for name in ("section", "seq", "batch"))
    sigma = (score_level[0].astype(jnp.float32) + 1.0) / LEVELS
    noised = (
        (1.0 - sigma) * samples[0].astype(jnp.float32) + sigma * noise[0].astype(jnp.float32)
    ).astype(jnp.bfloat16)
    source = jnp.where(section == 0, latent[0], jnp.where(section == 1, carried[0], noised))
    level = jnp.where(section >= 2, score_level[0], gen_level[0])
    modulated, gate = pick_modulate(source, mod_table[0], level)
    attended = attend(seqs, batches, qkv_weight[0], modulated, query_gain, key_gain)
    result, own_cols = project(
        sections, seqs, batches, attended, out_weight[0], source, gate[None], samples[0]
    )
    return (result[None, None], own_cols[None])


def solution(mesh):
    groups = mesh.shape["seq"] * mesh.shape["batch"]
    on_device = by_heads if HEADS % groups == 0 else by_batch
    return jax.shard_map(
        on_device,
        mesh=mesh,
        in_specs=(
            P("batch", "seq", None),
            P("batch", "seq", None),
            P("batch", "seq", None),
            P("batch", "seq", None),
            P("batch"),
            P("batch"),
            P("section", None, None, None),
            P("section", ("seq", "batch"), None),
            P("section", None, ("seq", "batch")),
            P("section", None),
            P("section", None),
        ),
        out_specs=(P("section", "batch", "seq", None), P("batch", "seq", "section")),
        check_vma=False,
    )
```
